32 devices in a mesh: groups: 2 (over y), owner: 4 (over z), tensor: 4 (over x, core).
Axes of the slice: x: 2, y: 2, z: 4, core: 2. Of those that a mesh axis runs over, the one named last changes fastest.
Arguments:
- requests: bfloat16 [384, 8192], P(('groups', 'owner'), 'tensor'), parts along dimension 0, may hold values from -6 to 6
- output_weight: bfloat16 [8192, 8192], P('tensor', 'owner'), may hold values from -0.0625 to 0.0625
- adapter_down_bank: bfloat16 [48, 8192, 64], P(('groups', 'owner'), 'tensor'), parts along dimension 0, may hold values from -0.0625 to 0.0625
- adapter_up_bank: bfloat16 [48, 64, 8192], P(('groups', 'owner'), None, 'tensor'), parts along dimension 0, may hold values from -0.75 to 0.75
- request_adapter: int32 [384], P(('groups', 'owner')), parts along dimension 0, may hold values from 0 to 23, as said below
- adapter_position: int32 [48], P('groups'), parts along dimension 0, may hold values from 0 to 23, as said below
Outputs:
- projected: bfloat16 [384, 8192], P(('groups', 'owner'), 'tensor'), parts along dimension 0
The draws below stay inside these ranges and needn't reach their ends.
There are 2 independent parts, one for each index of `groups`. The reference program is written for one: setup_inputs(seed, part) draws one part's arguments, and reference() takes and returns one part's arrays. A program takes and returns all parts, laid end to end along the dimension named above; an argument that names none is the same for every part. Nothing has to cross between parts.
Inputs may be any that keep to these rules, and one draw needn't show every extreme that they name: `request_adapter`: adapter a sits in bank position adapter_position[a]; position p belongs to owner index p // 6. Among the 48 requests of one owner index (aligned blocks of rows), at most 24 name adapters of one owner; in every draw one owner is named by exactly 24 requests of every block. `adapter_position`: A permutation: each bank position once.
All inputs are finite; a program needn't handle non-finite values.
Results may differ from the reference program's by a relative error of at most 0.005.
Values may be sent and summed in bfloat16 or wider, within the bound.
A program may use at most 64 MiB of HBM per device.

```python
import jax
import jax.numpy as jnp
from jax import lax

MODEL_WIDTH = 8192
ADAPTER_RANK = 64
ROWS_DEV = 48
ADP_DEV = 6
CAP = 24
TOKENS = 192
ADAPTER_TOTAL = 24


def routing(key):
    key = jax.random.fold_in(key, 11)
    block_count = TOKENS // ROWS_DEV
    owner_count = ADAPTER_TOTAL // ADP_DEV
    spare = ROWS_DEV - CAP
    key_place, key_hot, key_other, key_shuffle, key_slot = jax.random.split(key, 5)
    position = jax.random.permutation(key_place, ADAPTER_TOTAL)
    hottest = jax.random.randint(key_hot, (), 0, owner_count)
    others = jax.vmap(lambda k: jax.random.permutation(k, owner_count - 1))(jax.random.split(key_other, block_count))
    column = jnp.broadcast_to((jnp.arange(spare) % (owner_count - 1))[None, :], (block_count, spare))
    chosen = jnp.take_along_axis(others, column, 1)
    chosen = (hottest + 1 + chosen) % owner_count
    owners_blk = jnp.concatenate([jnp.full((block_count, CAP), hottest), chosen], 1)
    shuffle = jax.vmap(lambda k: jax.random.permutation(k, ROWS_DEV))(jax.random.split(key_shuffle, block_count))
    owners_blk = jnp.take_along_axis(owners_blk, shuffle, 1)
    slot_rows = jax.random.randint(key_slot, (block_count, ROWS_DEV), 0, ADP_DEV)
    wanted_pos = owners_blk * ADP_DEV + slot_rows
    inverse = jnp.argsort(position, stable=True)
    adapter_rows = inverse[wanted_pos].reshape(TOKENS)
    return (adapter_rows.astype(jnp.int32), position.astype(jnp.int32))


def draw_request_adapter(key, part):
    return routing(key)[0]


def draw_adapter_position(key, part):
    return routing(key)[1]


def block_levels(key, extent, shards, low, top_value):
    def one(dim, parts):
        heights = jax.random.uniform(jax.random.fold_in(jax.random.fold_in(key, 6), dim), (parts,), jnp.float32, low / len(shards), top_value / len(shards))
        return jnp.repeat(jnp.exp(heights), extent[dim] // parts).reshape((-1,) + (1,) * (len(extent) - dim - 1))

    level = one(*shards[0])
    for cut in shards[1:]:
        level = level * one(*cut)
    return level


def noise(rng, dims, width, most, shards=(), held_as=jnp.bfloat16):
    gain = block_levels(rng, dims, shards, -0.22, 0.18) if shards else 1.0
    entries = jax.random.normal(rng, dims, jnp.float32) * width * gain
    return jnp.minimum(jnp.maximum(entries, -most), most).astype(held_as)


def setup_inputs(seed: int = 0, part: int = 0) -> dict:
    keys = jax.random.split(jax.random.key(seed), 7)
    own_keys = jax.random.split(jax.random.fold_in(keys[6], part), 7)
    return {
        "requests": noise(own_keys[0], (TOKENS, MODEL_WIDTH), 1.0, 6.0, ((0, 4), (1, 4))),
        "output_weight": noise(keys[1], (MODEL_WIDTH, MODEL_WIDTH), MODEL_WIDTH ** -0.5, 0.0625, ((0, 4), (1, 4))),
        "adapter_down_bank": noise(own_keys[2], (ADAPTER_TOTAL, MODEL_WIDTH, ADAPTER_RANK), MODEL_WIDTH ** -0.5, 0.0625, ((0, 4), (1, 4))),
        "adapter_up_bank": noise(own_keys[3], (ADAPTER_TOTAL, ADAPTER_RANK, MODEL_WIDTH), ADAPTER_RANK ** -0.5, 0.75, ((0, 4), (2, 4))),
        "request_adapter": draw_request_adapter(jax.random.fold_in(jax.random.fold_in(keys[6], part), 71), part),
        "adapter_position": draw_adapter_position(jax.random.fold_in(jax.random.fold_in(keys[6], part), 71), part),
    }


def reference(requests, output_weight, adapter_down_bank, adapter_up_bank, request_adapter, adapter_position):
    base_out = jnp.dot(requests, output_weight, preferred_element_type=jnp.float32)
    position = adapter_position[request_adapter].astype(jnp.int32)
    blocks_x = requests.reshape(TOKENS // ROWS_DEV, ROWS_DEV, MODEL_WIDTH)
    blocks_p = position.reshape(TOKENS // ROWS_DEV, ROWS_DEV)

    def one_block(block_pair):
        block_rows, location_index = block_pair
        down_matrix_rows = adapter_down_bank[location_index].astype(jnp.float32)
        low_rank = jnp.einsum("rf,rfk->rk", block_rows.astype(jnp.float32), down_matrix_rows, precision=lax.Precision.HIGHEST).astype(jnp.bfloat16)
        low_rank = lax.optimization_barrier(low_rank)
        up_matrix_rows = adapter_up_bank[location_index].astype(jnp.float32)
        return jnp.einsum("rk,rkf->rf", low_rank.astype(jnp.float32), up_matrix_rows, precision=lax.Precision.HIGHEST).astype(jnp.bfloat16)

    delta_rows = lax.map(one_block, (blocks_x, blocks_p)).reshape(TOKENS, MODEL_WIDTH)
    return (base_out + delta_rows.astype(jnp.float32)).astype(jnp.bfloat16)
```

```python
import functools

import jax
import jax.numpy as jnp
from jax import lax
from jax.experimental import pallas as pl
from jax.experimental.pallas import tpu as pltpu
from jax.sharding import PartitionSpec as P


def general(
    requests, output_weight, adapter_down_bank, adapter_up_bank, request_adapter, adapter_position
):
    rows_dev, features = requests.shape
    owners = lax.axis_size("owner")
    bank_capacity = adapter_down_bank.shape[0]
    most_rows = max(2, (2 * rows_dev + owners - 1) // owners)
    slot_count = owners * most_rows
    gathered = lax.all_gather(requests, "owner", axis=0, tiled=True)
    partial_sum = jnp.dot(gathered, output_weight, preferred_element_type=jnp.float32)
    spread = lax.all_to_all(partial_sum, "owner", split_axis=0, concat_axis=1, tiled=True)
    base_out = lax.psum_scatter(spread, "tensor", scatter_dimension=1, tiled=True)
    adapter_rows = jnp.arange(adapter_position.shape[0], dtype=jnp.int32)
    matched = request_adapter[:, None] == adapter_rows[None, :]
    position = jnp.sum(jnp.where(matched, adapter_position[None, :], 0), axis=1)
    owner_of = position // bank_capacity
    slot_of = position % bank_capacity
    count_rows = owner_of.shape[-1]
    same_owner = owner_of[..., :, None] == owner_of[..., None, :]
    before = jnp.arange(count_rows)[None, :] < jnp.arange(count_rows)[:, None]
    target = owner_of * most_rows + jnp.sum(same_owner & before, axis=-1)
    picker = target[None, :] == jnp.arange(slot_count)[:, None]
    outgoing = jnp.dot(
        picker.astype(jnp.bfloat16), requests, preferred_element_type=jnp.float32
    ).astype(jnp.bfloat16)
    slot_tags = jnp.sum(jnp.where(picker, slot_of[None, :] + 1, 0), axis=1)
    received_rows, arrived_tags = (
        lax.all_to_all(
            outgoing.reshape(owners, most_rows, features),
            "owner",
            split_axis=0,
            concat_axis=0,
            tiled=True,
        ),
        lax.all_to_all(
            slot_tags.reshape(owners, most_rows), "owner", split_axis=0, concat_axis=0, tiled=True
        ),
    )
    received_rows = received_rows.reshape(slot_count, features)
    arrived_tags = arrived_tags.reshape(slot_count)
    select = arrived_tags[:, None] == jnp.arange(1, bank_capacity + 1)[None, :]
    complete_low_rank = jnp.einsum(
        "jw,bwo->jbo", received_rows, adapter_down_bank, preferred_element_type=jnp.float32
    )
    partial_low = jnp.sum(jnp.where(select[:, :, None], complete_low_rank, 0.0), axis=1)
    summed = lax.psum(partial_low, "tensor").astype(jnp.bfloat16)
    scattered_low_rank = jnp.where(
        select[:, :, None], summed[:, None, :], jnp.zeros((), jnp.bfloat16)
    )
    delta_rows = jnp.einsum(
        "vtj,tje->ve", scattered_low_rank, adapter_up_bank, preferred_element_type=jnp.float32
    ).astype(jnp.bfloat16)
    returned_rows = lax.all_to_all(
        delta_rows.reshape(owners, most_rows, delta_rows.shape[1]),
        "owner",
        split_axis=0,
        concat_axis=0,
        tiled=True,
    )
    returned_rows = returned_rows.reshape(slot_count, delta_rows.shape[1])
    own_delta = jnp.dot(
        picker.T.astype(jnp.bfloat16), returned_rows, preferred_element_type=jnp.float32
    )
    return (base_out + own_delta).astype(jnp.bfloat16)


MESH = pl.DeviceIdType.MESH
F32, BF16 = jnp.float32, jnp.bfloat16
LANES = 128


def dot(a, b, dims=((1,), (0,))):
    return lax.dot_general(a, b, (dims, ((), ())), preferred_element_type=F32)


def kernel(
    n, bank, rank, cap, tile,
    x_hbm, meta_hbm, w_hbm, down_hbm, up_hbm, out_ref,
    xg, w, down, up, low, part, parts_in, acc, swap, swap_in, delta_out, delta_in,
    local_sem, up_send, dn_send, x_recv, low_send, low_recv, rs_send, rs_recv,
    delta_send, delta_recv, swap_send, swap_recv,
):
    g, o, t = lax.axis_index("groups"), lax.axis_index("owner"), lax.axis_index("tensor")
    rows, width = x_hbm.shape
    cols = w.shape[1]
    half = cols // 2
    copies = bank * rank // LANES

    def local(src, dst, i):
        return pltpu.make_async_copy(src, dst, local_sem.at[i])

    loads = [
        local(x_hbm, xg.at[o, :, pl.ds(0, width)], 0),
        local(meta_hbm, xg.at[o, :, pl.ds(width, 2 * LANES)], 1),
        local(down_hbm, down, 2),
        local(w_hbm, w, 3),
        local(up_hbm, up, 4),
    ]
    for load in loads:
        load.start()

    barrier = pltpu.get_barrier_semaphore()
    for s in range(1, n):
        pl.semaphore_signal(barrier, inc=1, device_id=(g, lax.rem(o + s, n), t), device_id_type=MESH)
        pl.semaphore_signal(barrier, inc=1, device_id=(g, o, lax.rem(t + s, n)), device_id_type=MESH)

    @pl.when(o != t)
    def _():
        pl.semaphore_signal(barrier, inc=1, device_id=(g, t, o), device_id_type=MESH)

    pl.semaphore_wait(barrier, 2 * (n - 1) + jnp.where(o != t, 1, 0))
    loads[0].wait()
    loads[1].wait()

    def remote(src, dst, send, recv, device):
        return pltpu.make_async_remote_copy(
            src_ref=src, dst_ref=dst, send_sem=send, recv_sem=recv, device_id=device, device_id_type=MESH
        )

    def x_up(b):
        return remote(xg.at[b], xg.at[b], up_send.at[b], x_recv.at[b], (g, jnp.minimum(o + 1, n - 1), t))

    def x_down(b):
        return remote(xg.at[b], xg.at[b], dn_send.at[b], x_recv.at[b], (g, jnp.maximum(o - 1, 0), t))

    def low_copy(b, to, src):
        return remote(low.at[b, src], low.at[b, src], low_send.at[b, to], low_recv.at[b, src], (g, o, to))

    def part_copy(b, src):
        return remote(part.at[b], parts_in.at[src], rs_send.at[b], rs_recv.at[src], (g, o, b))

    def delta_copy(b, src):
        return remote(
            delta_out.at[b], delta_in.at[pl.ds(src * 2 * cap, 2 * cap)], delta_send.at[b], delta_recv.at[src], (g, b, t)
        )

    def swap_copy():
        return remote(swap, swap_in, swap_send, swap_recv, (g, t, o))

    mirrored = 2 * o >= n
    near = jnp.where(mirrored, n - 1 - o, o)

    def order(k):
        inner = jnp.where(k % 2 == 1, near - (k + 1) // 2, near + k // 2)
        b = jnp.where(k <= 2 * near, inner, k)
        return jnp.where(mirrored, n - 1 - b, b)

    def finish_parts():
        for s in range(1, n):
            part_copy(t, lax.rem(t + s, n)).wait_recv()

        @pl.loop(0, cols // tile)
        def _(c):
            at = pl.ds(pl.multiple_of(c * tile, tile), tile)
            total = acc[:, at]
            for s in range(1, n):
                total += parts_in[lax.rem(t + s, n), :, at].astype(F32)
            acc[:, at] = total
            swap[:, at] = total.astype(BF16)

        @pl.when(o != t)
        def _():
            swap_copy().start()

    def block(k, carry):
        b = order(k)

        @pl.when(k > 0)
        def _():
            x_up(b).wait_recv()

        @pl.when((o < n - 1) & (b <= o))
        def _():
            x_up(b).start()

        @pl.when((o > 0) & (b >= o))
        def _():
            x_down(b).start()

        @pl.when(k == 0)
        def _():
            loads[2].wait()

        place = xg[b, :, width : width + LANES].astype(F32)
        target = xg[b, :, width + LANES : width + 2 * LANES].astype(F32)
        lane = lax.broadcasted_iota(jnp.int32, (rows, bank * rank), 1)
        mine = jnp.concatenate([place] * copies, axis=1) == (lane // rank + o * bank).astype(F32)
        every = jnp.where(mine, dot(xg[b, :, :width], down[...], ((1,), (1,))), 0.0)
        folded = every[:, :LANES]
        for i in range(1, copies):
            folded += every[:, i * LANES : (i + 1) * LANES]
        low[b, t] = folded + pltpu.roll(folded, rank, 1)
        for s in range(1, n):
            low_copy(b, lax.rem(t + s, n), t).start()

        @pl.when(k == 0)
        def _():
            loads[3].wait()

        @pl.loop(0, cols // tile)
        def _(c):
            at = pl.ds(pl.multiple_of(c * tile, tile), tile)
            value = dot(xg[b, :, :width], w[:, at])
            part[b, :, at] = value.astype(BF16)

            @pl.when(b == t)
            def _():
                acc[:, at] = value

        @pl.when(b != t)
        def _():
            part_copy(b, t).start()

        @pl.when(k == 0)
        def _():
            loads[4].wait()

        for s in range(1, n):
            low_copy(b, t, lax.rem(t + s, n)).wait_recv()
        total = low[b, 0]
        for s in range(1, n):
            total += low[b, s]
        spread = jnp.where(mine, jnp.concatenate([total] * copies, axis=1), 0.0).astype(BF16)
        slot = lax.broadcasted_iota(jnp.int32, (rows, LANES), 1)
        picker = (target == (slot + o * cap).astype(F32)) & (slot < cap)
        packed = dot(picker.astype(F32).astype(BF16), spread, ((0,), (0,)))[:cap].astype(BF16)
        made = jnp.concatenate([dot(packed, up[:, :half]), dot(packed, up[:, half:])], axis=0).astype(BF16)

        @pl.when(b == o)
        def _():
            delta_in[pl.ds(pl.multiple_of(o * 2 * cap, 2 * cap), 2 * cap), :] = made

        @pl.when(b != o)
        def _():
            delta_out[b] = made
            delta_copy(b, o).start()

        @pl.when((k > 0) & (order(jnp.maximum(k - 1, 0)) == t))
        def _():
            finish_parts()

        return carry

    lax.fori_loop(0, n, block, 0)

    @pl.when(order(n - 1) == t)
    def _():
        finish_parts()

    for s in range(1, n):
        delta_copy(o, lax.rem(o + s, n)).wait_recv()

    @pl.when(o != t)
    def _():
        swap_copy().wait_recv()
        acc[...] = swap_in[...].astype(F32)

    target = xg[o, :, width + LANES : width + LANES + 1].astype(F32).astype(jnp.int32)
    wanted = target + target // cap * cap
    slot = lax.broadcasted_iota(jnp.int32, (rows, n * 2 * cap), 1)
    for h in range(2):
        unpick = (slot == wanted + h * cap).astype(F32).astype(BF16)
        at = slice(h * half, (h + 1) * half)
        out_ref[:, at] = (acc[:, at] + dot(unpick, delta_in[...])).astype(BF16)

    def drain(b, carry):
        @pl.when((o < n - 1) & (b <= o))
        def _():
            x_up(b).wait_send()

        @pl.when((o > 0) & (b >= o))
        def _():
            x_down(b).wait_send()

        @pl.when(b != t)
        def _():
            part_copy(b, t).wait_send()

        @pl.when(b != o)
        def _():
            delta_copy(b, o).wait_send()

        for s in range(1, n):
            low_copy(b, lax.rem(t + s, n), t).wait_send()
        return carry

    lax.fori_loop(0, n, drain, 0)

    @pl.when(o != t)
    def _():
        swap_copy().wait_send()


def fused(
    requests, output_weight, adapter_down_bank, adapter_up_bank, request_adapter, adapter_position
):
    rows, width = requests.shape
    n = lax.axis_size("owner")
    cols = output_weight.shape[1]
    bank, rank = adapter_down_bank.shape[0], adapter_down_bank.shape[2]
    cap = max(2, (2 * rows + n - 1) // n)
    adapters = jnp.arange(adapter_position.shape[0], dtype=jnp.int32)
    matched = request_adapter[:, None] == adapters[None, :]
    position = jnp.sum(jnp.where(matched, adapter_position[None, :], 0), axis=1)
    owner_of = position // bank
    before = jnp.arange(rows)[None, :] < jnp.arange(rows)[:, None]
    same = owner_of[:, None] == owner_of[None, :]
    target = owner_of * cap + jnp.sum(same & before, axis=-1)
    meta = jnp.where(jnp.arange(2 * LANES)[None, :] < LANES, position[:, None], target[:, None]).astype(BF16)
    down = jnp.swapaxes(adapter_down_bank, 1, 2).reshape(bank * rank, width)
    up = adapter_up_bank.reshape(bank * rank, cols)
    anywhere = pl.BlockSpec(memory_space=pl.ANY)
    dma = pltpu.SemaphoreType.DMA
    return pl.pallas_call(
        functools.partial(kernel, n, bank, rank, cap, 512),
        out_shape=jax.ShapeDtypeStruct((rows, cols), BF16),
        in_specs=[anywhere] * 5,
        out_specs=pl.BlockSpec(memory_space=pltpu.VMEM),
        scratch_shapes=[
            pltpu.VMEM((n, rows, width + 2 * LANES), BF16),
            pltpu.VMEM((width, cols), BF16),
            pltpu.VMEM((bank * rank, width), BF16),
            pltpu.VMEM((bank * rank, cols), BF16),
            pltpu.VMEM((n, n, rows, LANES), F32),
            pltpu.VMEM((n, rows, cols), BF16),
            pltpu.VMEM((n, rows, cols), BF16),
            pltpu.VMEM((rows, cols), F32),
            pltpu.VMEM((rows, cols), BF16),
            pltpu.VMEM((rows, cols), BF16),
            pltpu.VMEM((n, 2 * cap, cols // 2), BF16),
            pltpu.VMEM((n * 2 * cap, cols // 2), BF16),
            dma((5,)), dma((n,)), dma((n,)), dma((n,)), dma((n, n)), dma((n, n)), dma((n,)), dma((n,)),
            dma((n,)), dma((n,)), dma, dma,
        ],
        compiler_params=pltpu.CompilerParams(
            collective_id=0, has_side_effects=True, vmem_limit_bytes=60 * 2**20
        ),
    )(requests, meta, output_weight, down, up)


def shards(
    requests, output_weight, adapter_down_bank, adapter_up_bank, request_adapter, adapter_position
):
    arguments = (
        requests, output_weight, adapter_down_bank, adapter_up_bank, request_adapter, adapter_position
    )
    rows, width = requests.shape
    owners, pieces = lax.axis_size("owner"), lax.axis_size("tensor")
    bank, rank = adapter_down_bank.shape[0], adapter_down_bank.shape[2]
    cap = max(2, (2 * rows + owners - 1) // owners)
    fits = (
        owners == pieces
        and output_weight.shape[1] % 512 == 0
        and 2 * rank == LANES
        and bank * rank % LANES == 0
        and rows % 16 == 0
        and cap % 8 == 0
        and cap <= LANES
        and owners * max(bank, cap) <= 256
    )
    return fused(*arguments) if fits else general(*arguments)


def solution(mesh):
    placed = (
        P(("groups", "owner"), "tensor"),
        P("tensor", "owner"),
        P(("groups", "owner"), "tensor", None),
        P(("groups", "owner"), None, "tensor"),
        P(("groups", "owner")),
        P("groups"),
    )
    return jax.shard_map(
        shards,
        mesh=mesh,
        in_specs=placed,
        out_specs=P(("groups", "owner"), "tensor"),
        check_vma=False,
    )
```

```python
import functools

import jax
import jax.numpy as jnp
from jax import lax
from jax.experimental import pallas as pl
from jax.experimental.pallas import tpu as pltpu
from jax.sharding import PartitionSpec as P


def general(
    requests, output_weight, adapter_down_bank, adapter_up_bank, request_adapter, adapter_position
):
    rows_dev, features = requests.shape
    owners = lax.axis_size("owner")
    bank_capacity = adapter_down_bank.shape[0]
    most_rows = max(2, (2 * rows_dev + owners - 1) // owners)
    slot_count = owners * most_rows
    gathered = lax.all_gather(requests, "owner", axis=0, tiled=True)
    partial_sum = jnp.dot(gathered, output_weight, preferred_element_type=jnp.float32)
    spread = lax.all_to_all(partial_sum, "owner", split_axis=0, concat_axis=1, tiled=True)
    base_out = lax.psum_scatter(spread, "tensor", scatter_dimension=1, tiled=True)
    adapter_rows = jnp.arange(adapter_position.shape[0], dtype=jnp.int32)
    matched = request_adapter[:, None] == adapter_rows[None, :]
    position = jnp.sum(jnp.where(matched, adapter_position[None, :], 0), axis=1)
    owner_of = position // bank_capacity
    slot_of = position % bank_capacity
    count_rows = owner_of.shape[-1]
    same_owner = owner_of[..., :, None] == owner_of[..., None, :]
    before = jnp.arange(count_rows)[None, :] < jnp.arange(count_rows)[:, None]
    target = owner_of * most_rows + jnp.sum(same_owner & before, axis=-1)
    picker = target[None, :] == jnp.arange(slot_count)[:, None]
    outgoing = jnp.dot(
        picker.astype(jnp.bfloat16), requests, preferred_element_type=jnp.float32
    ).astype(jnp.bfloat16)
    slot_tags = jnp.sum(jnp.where(picker, slot_of[None, :] + 1, 0), axis=1)
    received_rows, arrived_tags = (
        lax.all_to_all(
            outgoing.reshape(owners, most_rows, features),
            "owner",
            split_axis=0,
            concat_axis=0,
            tiled=True,
        ),
        lax.all_to_all(
            slot_tags.reshape(owners, most_rows), "owner", split_axis=0, concat_axis=0, tiled=True
        ),
    )
    received_rows = received_rows.reshape(slot_count, features)
    arrived_tags = arrived_tags.reshape(slot_count)
    select = arrived_tags[:, None] == jnp.arange(1, bank_capacity + 1)[None, :]
    complete_low_rank = jnp.einsum(
        "jw,bwo->jbo", received_rows, adapter_down_bank, preferred_element_type=jnp.float32
    )
    partial_low = jnp.sum(jnp.where(select[:, :, None], complete_low_rank, 0.0), axis=1)
    summed = lax.psum(partial_low, "tensor").astype(jnp.bfloat16)
    scattered_low_rank = jnp.where(
        select[:, :, None], summed[:, None, :], jnp.zeros((), jnp.bfloat16)
    )
    delta_rows = jnp.einsum(
        "vtj,tje->ve", scattered_low_rank, adapter_up_bank, preferred_element_type=jnp.float32
    ).astype(jnp.bfloat16)
    returned_rows = lax.all_to_all(
        delta_rows.reshape(owners, most_rows, delta_rows.shape[1]),
        "owner",
        split_axis=0,
        concat_axis=0,
        tiled=True,
    )
    returned_rows = returned_rows.reshape(slot_count, delta_rows.shape[1])
    own_delta = jnp.dot(
        picker.T.astype(jnp.bfloat16), returned_rows, preferred_element_type=jnp.float32
    )
    return (base_out + own_delta).astype(jnp.bfloat16)


MESH = pl.DeviceIdType.MESH
F32, BF16 = jnp.float32, jnp.bfloat16
LANES = 128


def dot(a, b, dims=((1,), (0,))):
    return lax.dot_general(a, b, (dims, ((), ())), preferred_element_type=F32)


def kernel(
    n, bank, rank, cap, tile,
    x_hbm, named_ref, place_ref, w_hbm, down_hbm, up_hbm, out_ref,
    xg, w, down, up, low, part, parts_in, acc, swap, swap_in, delta_out, delta_in,
    local_sem, up_send, dn_send, x_recv, low_send, low_recv, rs_send, rs_recv,
    delta_send, delta_recv, swap_send, swap_recv,
):
    g, o, t = lax.axis_index("groups"), lax.axis_index("owner"), lax.axis_index("tensor")
    rows, width = x_hbm.shape
    cols = w.shape[1]
    half = cols // 2
    copies = bank * rank // LANES

    def local(src, dst, i):
        return pltpu.make_async_copy(src, dst, local_sem.at[i])

    loads = [
        local(x_hbm, xg.at[o, :, pl.ds(0, width)], 0),
        local(down_hbm, down, 1),
        local(w_hbm, w, 2),
        local(up_hbm, up, 3),
    ]
    for load in loads:
        load.start()

    barrier = pltpu.get_barrier_semaphore()
    for s in range(1, n):
        pl.semaphore_signal(barrier, inc=1, device_id=(g, lax.rem(o + s, n), t), device_id_type=MESH)
        pl.semaphore_signal(barrier, inc=1, device_id=(g, o, lax.rem(t + s, n)), device_id_type=MESH)

    @pl.when(o != t)
    def _():
        pl.semaphore_signal(barrier, inc=1, device_id=(g, t, o), device_id_type=MESH)

    down_rows = lax.broadcasted_iota(jnp.int32, (rows, rows), 0)
    across = lax.broadcasted_iota(jnp.int32, (rows, rows), 1)
    same_row = down_rows == across
    named = jnp.sum(jnp.where(same_row, named_ref[...].astype(F32), 0.0), axis=1, keepdims=True)
    adapters = lax.broadcasted_iota(jnp.int32, (rows, place_ref.shape[1]), 1).astype(F32)
    places = jnp.sum(jnp.where(named == adapters, place_ref[...].astype(F32), 0.0), axis=1, keepdims=True)
    holder = sum(jnp.where(places >= float(i * bank), 1.0, 0.0) for i in range(1, n))
    holder_row = jnp.sum(jnp.where(same_row, holder, 0.0), axis=0, keepdims=True)
    earlier = jnp.sum(jnp.where((holder == holder_row) & (across < down_rows), 1.0, 0.0), axis=1, keepdims=True)
    targets = holder * cap + earlier
    wide = (rows, LANES)
    xg[o, :, width : width + LANES] = jnp.broadcast_to(places, wide).astype(BF16)
    xg[o, :, width + LANES : width + 2 * LANES] = jnp.broadcast_to(targets, wide).astype(BF16)
    pl.semaphore_wait(barrier, 2 * (n - 1) + jnp.where(o != t, 1, 0))
    loads[0].wait()

    def remote(src, dst, send, recv, device):
        return pltpu.make_async_remote_copy(
            src_ref=src, dst_ref=dst, send_sem=send, recv_sem=recv, device_id=device, device_id_type=MESH
        )

    def x_up(b):
        return remote(xg.at[b], xg.at[b], up_send.at[b], x_recv.at[b], (g, jnp.minimum(o + 1, n - 1), t))

    def x_down(b):
        return remote(xg.at[b], xg.at[b], dn_send.at[b], x_recv.at[b], (g, jnp.maximum(o - 1, 0), t))

    def low_copy(b, to, src):
        return remote(low.at[b, src], low.at[b, src], low_send.at[b, to], low_recv.at[b, src], (g, o, to))

    def part_copy(b, src, h):
        return remote(part.at[b, h], parts_in.at[src, h], rs_send.at[b, h], rs_recv.at[src, h], (g, o, b))

    def delta_copy(b, src):
        return remote(
            delta_out.at[b], delta_in.at[pl.ds(src * 2 * cap, 2 * cap)], delta_send.at[b], delta_recv.at[src], (g, b, t)
        )

    def swap_copy(h):
        return remote(swap.at[h], swap_in.at[h], swap_send.at[h], swap_recv.at[h], (g, t, o))

    mirrored = 2 * o >= n
    near = jnp.where(mirrored, n - 1 - o, o)

    def order(k):
        inner = jnp.where(k % 2 == 1, near - (k + 1) // 2, near + k // 2)
        b = jnp.where(k <= 2 * near, inner, k)
        return jnp.where(mirrored, n - 1 - b, b)

    def finish_parts():
        for h in range(2):
            for s in range(1, n):
                part_copy(t, lax.rem(t + s, n), h).wait_recv()
            total = acc[h]
            for s in range(1, n):
                total += parts_in[lax.rem(t + s, n), h].astype(F32)
            acc[h] = total
            swap[h] = total.astype(BF16)

            @pl.when(o != t)
            def _():
                swap_copy(h).start()

    def block(k, carry):
        b = order(k)

        below, above = jnp.maximum(o - k, 0), jnp.minimum(o + k, n - 1)

        @pl.when((k > 0) & (o - k >= 0))
        def _():
            x_up(below).wait_recv()

        @pl.when((o < n - 1) & (o - k >= 0))
        def _():
            x_up(below).start()

        @pl.when((k > 0) & (o + k < n))
        def _():
            x_up(above).wait_recv()

        @pl.when((o > 0) & (o + k < n))
        def _():
            x_down(above).start()

        @pl.when(k == 0)
        def _():
            loads[1].wait()

        place = xg[b, :, width : width + LANES].astype(F32)
        target = xg[b, :, width + LANES : width + 2 * LANES].astype(F32)
        lane = lax.broadcasted_iota(jnp.int32, (rows, bank * rank), 1)
        mine = jnp.concatenate([place] * copies, axis=1) == (lane // rank + o * bank).astype(F32)
        every = jnp.where(mine, dot(xg[b, :, :width], down[...], ((1,), (1,))), 0.0)
        folded = every[:, :LANES]
        for i in range(1, copies):
            folded += every[:, i * LANES : (i + 1) * LANES]
        low[b, t] = folded + pltpu.roll(folded, rank, 1)
        for s in range(1, n):
            low_copy(b, lax.rem(t + s, n), t).start()

        @pl.when(k == 0)
        def _():
            loads[2].wait()

        for h in range(2):

            @pl.loop(0, half // tile)
            def _(c):
                at = pl.ds(pl.multiple_of(c * tile, tile), tile)
                value = dot(xg[b, :, :width], w[:, pl.ds(pl.multiple_of(h * half + c * tile, tile), tile)])
                part[b, h, :, at] = value.astype(BF16)

                @pl.when(b == t)
                def _():
                    acc[h, :, at] = value

            @pl.when(b != t)
            def _():
                part_copy(b, t, h).start()

        @pl.when(k == 0)
        def _():
            loads[3].wait()

        for s in range(1, n):
            low_copy(b, t, lax.rem(t + s, n)).wait_recv()
        total = low[b, 0]
        for s in range(1, n):
            total += low[b, s]
        spread = jnp.where(mine, jnp.concatenate([total] * copies, axis=1), 0.0).astype(BF16)
        slot = lax.broadcasted_iota(jnp.int32, (rows, LANES), 1)
        picker = (target == (slot + o * cap).astype(F32)) & (slot < cap)
        packed = dot(picker.astype(F32).astype(BF16), spread, ((0,), (0,)))[:cap].astype(BF16)
        made = jnp.concatenate([dot(packed, up[:, :half]), dot(packed, up[:, half:])], axis=0).astype(BF16)

        @pl.when(b == o)
        def _():
            delta_in[pl.ds(pl.multiple_of(o * 2 * cap, 2 * cap), 2 * cap), :] = made

        @pl.when(b != o)
        def _():
            delta_out[b] = made
            delta_copy(b, o).start()

        @pl.when((k > 0) & (order(jnp.maximum(k - 1, 0)) == t))
        def _():
            finish_parts()

        return carry

    lax.fori_loop(0, n, block, 0)

    @pl.when(order(n - 1) == t)
    def _():
        finish_parts()

    for s in range(1, n):
        delta_copy(o, lax.rem(o + s, n)).wait_recv()

    target = xg[o, :, width + LANES : width + LANES + 1].astype(F32).astype(jnp.int32)
    wanted = target + target // cap * cap
    slot = lax.broadcasted_iota(jnp.int32, (rows, n * 2 * cap), 1)
    for h in range(2):
        unpick = (slot == wanted + h * cap).astype(F32).astype(BF16)
        own = dot(unpick, delta_in[...])

        @pl.when(o != t)
        def _():
            swap_copy(h).wait_recv()
            acc[h] = swap_in[h].astype(F32)

        out_ref[:, h * half : (h + 1) * half] = (acc[h] + own).astype(out_ref.dtype)

    def drain(b, carry):
        @pl.when((o < n - 1) & (b <= o))
        def _():
            x_up(b).wait_send()

        @pl.when((o > 0) & (b >= o))
        def _():
            x_down(b).wait_send()

        @pl.when(b != t)
        def _():
            part_copy(b, t, 0).wait_send()
            part_copy(b, t, 1).wait_send()

        @pl.when(b != o)
        def _():
            delta_copy(b, o).wait_send()

        for s in range(1, n):
            low_copy(b, lax.rem(t + s, n), t).wait_send()
        return carry

    lax.fori_loop(0, n, drain, 0)

    @pl.when(o != t)
    def _():
        swap_copy(0).wait_send()
        swap_copy(1).wait_send()


def fused(
    requests, output_weight, adapter_down_bank, adapter_up_bank, request_adapter, adapter_position
):
    rows, width = requests.shape
    n = lax.axis_size("owner")
    cols = output_weight.shape[1]
    bank, rank = adapter_down_bank.shape[0], adapter_down_bank.shape[2]
    cap = max(2, (2 * rows + n - 1) // n)
    down = jnp.swapaxes(adapter_down_bank, 1, 2).reshape(bank * rank, width)
    up = adapter_up_bank.reshape(bank * rank, cols)
    vmem = pl.BlockSpec(memory_space=pltpu.VMEM)
    anywhere = pl.BlockSpec(memory_space=pl.ANY)
    dma = pltpu.SemaphoreType.DMA
    return pl.pallas_call(
        functools.partial(kernel, n, bank, rank, cap, 512),
        out_shape=jax.ShapeDtypeStruct((rows, cols), BF16),
        in_specs=[anywhere, vmem, vmem, anywhere, anywhere, anywhere],
        out_specs=pl.BlockSpec(memory_space=pltpu.VMEM),
        scratch_shapes=[
            pltpu.VMEM((n, rows, width + 2 * LANES), BF16),
            pltpu.VMEM((width, cols), BF16),
            pltpu.VMEM((bank * rank, width), BF16),
            pltpu.VMEM((bank * rank, cols), BF16),
            pltpu.VMEM((n, n, rows, LANES), F32),
            pltpu.VMEM((n, 2, rows, cols // 2), BF16),
            pltpu.VMEM((n, 2, rows, cols // 2), BF16),
            pltpu.VMEM((2, rows, cols // 2), F32),
            pltpu.VMEM((2, rows, cols // 2), BF16),
            pltpu.VMEM((2, rows, cols // 2), BF16),
            pltpu.VMEM((n, 2 * cap, cols // 2), BF16),
            pltpu.VMEM((n * 2 * cap, cols // 2), BF16),
            dma((4,)), dma((n,)), dma((n,)), dma((n,)), dma((n, n)), dma((n, n)), dma((n, 2)), dma((n, 2)),
            dma((n,)), dma((n,)), dma((2,)), dma((2,)),
        ],
        compiler_params=pltpu.CompilerParams(
            collective_id=0, has_side_effects=True, vmem_limit_bytes=60 * 2**20
        ),
    )(requests, request_adapter[None], adapter_position[None], output_weight, down, up)


def shards(
    requests, output_weight, adapter_down_bank, adapter_up_bank, request_adapter, adapter_position
):
    arguments = (
        requests, output_weight, adapter_down_bank, adapter_up_bank, request_adapter, adapter_position
    )
    rows, width = requests.shape
    owners, pieces = lax.axis_size("owner"), lax.axis_size("tensor")
    bank, rank = adapter_down_bank.shape[0], adapter_down_bank.shape[2]
    cap = max(2, (2 * rows + owners - 1) // owners)
    fits = (
        owners == pieces
        and output_weight.shape[1] % 1024 == 0
        and 2 * rank == LANES
        and bank * rank % LANES == 0
        and rows % 16 == 0
        and cap % 8 == 0
        and cap <= LANES
        and owners * max(bank, cap) <= 256
        and adapter_position.shape[0] <= owners * bank
    )
    return fused(*arguments) if fits else general(*arguments)


def solution(mesh):
    placed = (
        P(("groups", "owner"), "tensor"),
        P("tensor", "owner"),
        P(("groups", "owner"), "tensor", None),
        P(("groups", "owner"), None, "tensor"),
        P(("groups", "owner")),
        P("groups"),
    )
    return jax.shard_map(
        shards,
        mesh=mesh,
        in_specs=placed,
        out_specs=P(("groups", "owner"), "tensor"),
        check_vma=False,
    )
```

```python
import functools

import jax
import jax.numpy as jnp
from jax import lax
from jax.experimental import pallas as pl
from jax.experimental.pallas import tpu as pltpu
from jax.sharding import PartitionSpec as P


def general(
    requests, output_weight, adapter_down_bank, adapter_up_bank, request_adapter, adapter_position
):
    rows_dev, features = requests.shape
    owners = lax.axis_size("owner")
    bank_capacity = adapter_down_bank.shape[0]
    most_rows = max(2, (2 * rows_dev + owners - 1) // owners)
    slot_count = owners * most_rows
    gathered = lax.all_gather(requests, "owner", axis=0, tiled=True)
    partial_sum = jnp.dot(gathered, output_weight, preferred_element_type=jnp.float32)
    spread = lax.all_to_all(partial_sum, "owner", split_axis=0, concat_axis=1, tiled=True)
    base_out = lax.psum_scatter(spread, "tensor", scatter_dimension=1, tiled=True)
    adapter_rows = jnp.arange(adapter_position.shape[0], dtype=jnp.int32)
    matched = request_adapter[:, None] == adapter_rows[None, :]
    position = jnp.sum(jnp.where(matched, adapter_position[None, :], 0), axis=1)
    owner_of = position // bank_capacity
    slot_of = position % bank_capacity
    count_rows = owner_of.shape[-1]
    same_owner = owner_of[..., :, None] == owner_of[..., None, :]
    before = jnp.arange(count_rows)[None, :] < jnp.arange(count_rows)[:, None]
    target = owner_of * most_rows + jnp.sum(same_owner & before, axis=-1)
    picker = target[None, :] == jnp.arange(slot_count)[:, None]
    outgoing = jnp.dot(
        picker.astype(jnp.bfloat16), requests, preferred_element_type=jnp.float32
    ).astype(jnp.bfloat16)
    slot_tags = jnp.sum(jnp.where(picker, slot_of[None, :] + 1, 0), axis=1)
    received_rows, arrived_tags = (
        lax.all_to_all(
            outgoing.reshape(owners, most_rows, features),
            "owner",
            split_axis=0,
            concat_axis=0,
            tiled=True,
        ),
        lax.all_to_all(
            slot_tags.reshape(owners, most_rows), "owner", split_axis=0, concat_axis=0, tiled=True
        ),
    )
    received_rows = received_rows.reshape(slot_count, features)
    arrived_tags = arrived_tags.reshape(slot_count)
    select = arrived_tags[:, None] == jnp.arange(1, bank_capacity + 1)[None, :]
    complete_low_rank = jnp.einsum(
        "jw,bwo->jbo", received_rows, adapter_down_bank, preferred_element_type=jnp.float32
    )
    partial_low = jnp.sum(jnp.where(select[:, :, None], complete_low_rank, 0.0), axis=1)
    summed = lax.psum(partial_low, "tensor").astype(jnp.bfloat16)
    scattered_low_rank = jnp.where(
        select[:, :, None], summed[:, None, :], jnp.zeros((), jnp.bfloat16)
    )
    delta_rows = jnp.einsum(
        "vtj,tje->ve", scattered_low_rank, adapter_up_bank, preferred_element_type=jnp.float32
    ).astype(jnp.bfloat16)
    returned_rows = lax.all_to_all(
        delta_rows.reshape(owners, most_rows, delta_rows.shape[1]),
        "owner",
        split_axis=0,
        concat_axis=0,
        tiled=True,
    )
    returned_rows = returned_rows.reshape(slot_count, delta_rows.shape[1])
    own_delta = jnp.dot(
        picker.T.astype(jnp.bfloat16), returned_rows, preferred_element_type=jnp.float32
    )
    return (base_out + own_delta).astype(jnp.bfloat16)


MESH = pl.DeviceIdType.MESH
F32, BF16 = jnp.float32, jnp.bfloat16
LANES = 128


def dot(a, b, dims=((1,), (0,))):
    return lax.dot_general(a, b, (dims, ((), ())), preferred_element_type=F32)


def kernel(
    n, bank, rank, cap, tile,
    x_hbm, named_ref, place_ref, w_hbm, down_hbm, up_hbm, out_ref,
    xg, w, down, up, low, part, parts_in, acc, swap, swap_in, delta_out, delta_in,
    local_sem, up_send, dn_send, x_recv, low_send, low_recv, rs_send, rs_recv,
    delta_send, delta_recv, swap_send, swap_recv,
):
    g, o, t = lax.axis_index("groups"), lax.axis_index("owner"), lax.axis_index("tensor")
    rows, width = x_hbm.shape
    cols = w.shape[1]
    half = cols // 2
    copies = bank * rank // LANES

    def local(src, dst, i):
        return pltpu.make_async_copy(src, dst, local_sem.at[i])

    loads = [
        local(x_hbm, xg.at[o, :, pl.ds(0, width)], 0),
        local(down_hbm, down, 1),
        local(w_hbm, w, 2),
        local(up_hbm, up, 3),
    ]
    for load in loads:
        load.start()

    barrier = pltpu.get_barrier_semaphore()
    for s in range(1, n):
        pl.semaphore_signal(barrier, inc=1, device_id=(g, lax.rem(o + s, n), t), device_id_type=MESH)
        pl.semaphore_signal(barrier, inc=1, device_id=(g, o, lax.rem(t + s, n)), device_id_type=MESH)

    @pl.when(o != t)
    def _():
        pl.semaphore_signal(barrier, inc=1, device_id=(g, t, o), device_id_type=MESH)

    down_rows = lax.broadcasted_iota(jnp.int32, (rows, rows), 0)
    across = lax.broadcasted_iota(jnp.int32, (rows, rows), 1)
    same_row = down_rows == across
    named = jnp.sum(jnp.where(same_row, named_ref[...].astype(F32), 0.0), axis=1, keepdims=True)
    adapters = lax.broadcasted_iota(jnp.int32, (rows, place_ref.shape[1]), 1).astype(F32)
    places = jnp.sum(jnp.where(named == adapters, place_ref[...].astype(F32), 0.0), axis=1, keepdims=True)
    holder = sum(jnp.where(places >= float(i * bank), 1.0, 0.0) for i in range(1, n))
    holder_row = jnp.sum(jnp.where(same_row, holder, 0.0), axis=0, keepdims=True)
    earlier = jnp.sum(jnp.where((holder == holder_row) & (across < down_rows), 1.0, 0.0), axis=1, keepdims=True)
    targets = holder * cap + earlier
    wide = (rows, LANES)
    xg[o, :, width : width + LANES] = jnp.broadcast_to(places, wide).astype(BF16)
    xg[o, :, width + LANES : width + 2 * LANES] = jnp.broadcast_to(targets, wide).astype(BF16)
    pl.semaphore_wait(barrier, 2 * (n - 1) + jnp.where(o != t, 1, 0))
    loads[0].wait()

    def remote(src, dst, send, recv, device):
        return pltpu.make_async_remote_copy(
            src_ref=src, dst_ref=dst, send_sem=send, recv_sem=recv, device_id=device, device_id_type=MESH
        )

    def x_up(b):
        return remote(xg.at[b], xg.at[b], up_send.at[b], x_recv.at[b], (g, jnp.minimum(o + 1, n - 1), t))

    def x_down(b):
        return remote(xg.at[b], xg.at[b], dn_send.at[b], x_recv.at[b], (g, jnp.maximum(o - 1, 0), t))

    def low_copy(b, to, src):
        return remote(low.at[b, src], low.at[b, src], low_send.at[b, to], low_recv.at[b, src], (g, o, to))

    def part_copy(b, src, h):
        return remote(part.at[b, h], parts_in.at[src, h], rs_send.at[b, h], rs_recv.at[src, h], (g, o, b))

    def delta_copy(b, src):
        return remote(
            delta_out.at[b], delta_in.at[pl.ds(src * 2 * cap, 2 * cap)], delta_send.at[b], delta_recv.at[src], (g, b, t)
        )

    def swap_copy(h):
        return remote(swap.at[h], swap_in.at[h], swap_send.at[h], swap_recv.at[h], (g, t, o))

    mirrored = 2 * o >= n
    near = jnp.where(mirrored, n - 1 - o, o)

    def order(k):
        inner = jnp.where(k % 2 == 1, near - (k + 1) // 2, near + k // 2)
        b = jnp.where(k <= 2 * near, inner, k)
        return jnp.where(mirrored, n - 1 - b, b)

    def finish_parts():
        for h in range(2):
            for s in range(1, n):
                part_copy(t, lax.rem(t + s, n), h).wait_recv()
            total = acc[h]
            for s in range(1, n):
                total += parts_in[lax.rem(t + s, n), h].astype(F32)
            acc[h] = total
            swap[h] = total.astype(BF16)

            @pl.when(o != t)
            def _():
                swap_copy(h).start()

    def routes(b):
        place = xg[b, :, width : width + LANES].astype(F32)
        target = xg[b, :, width + LANES : width + 2 * LANES].astype(F32)
        lane = lax.broadcasted_iota(jnp.int32, (rows, bank * rank), 1)
        mine = jnp.concatenate([place] * copies, axis=1) == (lane // rank + o * bank).astype(F32)
        return mine, target

    def finish_low(b):
        mine, target = routes(b)
        for s in range(1, n):
            low_copy(b, t, lax.rem(t + s, n)).wait_recv()
        total = low[b, 0]
        for s in range(1, n):
            total += low[b, s]
        spread = jnp.where(mine, jnp.concatenate([total] * copies, axis=1), 0.0).astype(BF16)
        slot = lax.broadcasted_iota(jnp.int32, (rows, LANES), 1)
        picker = (target == (slot + o * cap).astype(F32)) & (slot < cap)
        packed = dot(picker.astype(F32).astype(BF16), spread, ((0,), (0,)))[:cap].astype(BF16)
        made = jnp.concatenate([dot(packed, up[:, :half]), dot(packed, up[:, half:])], axis=0).astype(BF16)

        @pl.when(b == o)
        def _():
            delta_in[pl.ds(pl.multiple_of(o * 2 * cap, 2 * cap), 2 * cap), :] = made

        @pl.when(b != o)
        def _():
            delta_out[b] = made
            delta_copy(b, o).start()


    def block(k, carry):
        b = order(k)

        below, above = jnp.maximum(o - k, 0), jnp.minimum(o + k, n - 1)

        @pl.when((k > 0) & (o - k >= 0))
        def _():
            x_up(below).wait_recv()

        @pl.when((o < n - 1) & (o - k >= 0))
        def _():
            x_up(below).start()

        @pl.when((k > 0) & (o + k < n))
        def _():
            x_up(above).wait_recv()

        @pl.when((o > 0) & (o + k < n))
        def _():
            x_down(above).start()

        @pl.when(k == 0)
        def _():
            loads[1].wait()
            loads[3].wait()

        @pl.when(k > 0)
        def _():
            finish_low(order(jnp.maximum(k - 1, 0)))

        mine, _ = routes(b)
        every = jnp.where(mine, dot(xg[b, :, :width], down[...], ((1,), (1,))), 0.0)
        folded = every[:, :LANES]
        for i in range(1, copies):
            folded += every[:, i * LANES : (i + 1) * LANES]
        low[b, t] = folded + pltpu.roll(folded, rank, 1)
        for s in range(1, n):
            low_copy(b, lax.rem(t + s, n), t).start()

        @pl.when(k == 0)
        def _():
            loads[2].wait()

        for h in range(2):

            @pl.loop(0, half // tile)
            def _(c):
                at = pl.ds(pl.multiple_of(c * tile, tile), tile)
                value = dot(xg[b, :, :width], w[:, pl.ds(pl.multiple_of(h * half + c * tile, tile), tile)])
                part[b, h, :, at] = value.astype(BF16)

                @pl.when(b == t)
                def _():
                    acc[h, :, at] = value

            @pl.when(b != t)
            def _():
                part_copy(b, t, h).start()

        @pl.when((k > 0) & (order(jnp.maximum(k - 1, 0)) == t))
        def _():
            finish_parts()

        return carry

    lax.fori_loop(0, n, block, 0)
    finish_low(order(n - 1))

    @pl.when(order(n - 1) == t)
    def _():
        finish_parts()

    for s in range(1, n):
        delta_copy(o, lax.rem(o + s, n)).wait_recv()

    target = xg[o, :, width + LANES : width + LANES + 1].astype(F32).astype(jnp.int32)
    wanted = target + target // cap * cap
    slot = lax.broadcasted_iota(jnp.int32, (rows, n * 2 * cap), 1)
    for h in range(2):
        unpick = (slot == wanted + h * cap).astype(F32).astype(BF16)
        own = dot(unpick, delta_in[...])

        @pl.when(o != t)
        def _():
            swap_copy(h).wait_recv()
            acc[h] = swap_in[h].astype(F32)

        out_ref[:, h * half : (h + 1) * half] = (acc[h] + own).astype(out_ref.dtype)

    def drain(b, carry):
        @pl.when((o < n - 1) & (b <= o))
        def _():
            x_up(b).wait_send()

        @pl.when((o > 0) & (b >= o))
        def _():
            x_down(b).wait_send()

        @pl.when(b != t)
        def _():
            part_copy(b, t, 0).wait_send()
            part_copy(b, t, 1).wait_send()

        @pl.when(b != o)
        def _():
            delta_copy(b, o).wait_send()

        for s in range(1, n):
            low_copy(b, lax.rem(t + s, n), t).wait_send()
        return carry

    lax.fori_loop(0, n, drain, 0)

    @pl.when(o != t)
    def _():
        swap_copy(0).wait_send()
        swap_copy(1).wait_send()


def fused(
    requests, output_weight, adapter_down_bank, adapter_up_bank, request_adapter, adapter_position
):
    rows, width = requests.shape
    n = lax.axis_size("owner")
    cols = output_weight.shape[1]
    bank, rank = adapter_down_bank.shape[0], adapter_down_bank.shape[2]
    cap = max(2, (2 * rows + n - 1) // n)
    down = jnp.swapaxes(adapter_down_bank, 1, 2).reshape(bank * rank, width)
    up = adapter_up_bank.reshape(bank * rank, cols)
    vmem = pl.BlockSpec(memory_space=pltpu.VMEM)
    anywhere = pl.BlockSpec(memory_space=pl.ANY)
    dma = pltpu.SemaphoreType.DMA
    return pl.pallas_call(
        functools.partial(kernel, n, bank, rank, cap, 512),
        out_shape=jax.ShapeDtypeStruct((rows, cols), BF16),
        in_specs=[anywhere, vmem, vmem, anywhere, anywhere, anywhere],
        out_specs=pl.BlockSpec(memory_space=pltpu.VMEM),
        scratch_shapes=[
            pltpu.VMEM((n, rows, width + 2 * LANES), BF16),
            pltpu.VMEM((width, cols), BF16),
            pltpu.VMEM((bank * rank, width), BF16),
            pltpu.VMEM((bank * rank, cols), BF16),
            pltpu.VMEM((n, n, rows, LANES), F32),
            pltpu.VMEM((n, 2, rows, cols // 2), BF16),
            pltpu.VMEM((n, 2, rows, cols // 2), BF16),
            pltpu.VMEM((2, rows, cols // 2), F32),
            pltpu.VMEM((2, rows, cols // 2), BF16),
            pltpu.VMEM((2, rows, cols // 2), BF16),
            pltpu.VMEM((n, 2 * cap, cols // 2), BF16),
            pltpu.VMEM((n * 2 * cap, cols // 2), BF16),
            dma((4,)), dma((n,)), dma((n,)), dma((n,)), dma((n, n)), dma((n, n)), dma((n, 2)), dma((n, 2)),
            dma((n,)), dma((n,)), dma((2,)), dma((2,)),
        ],
        compiler_params=pltpu.CompilerParams(
            collective_id=0, has_side_effects=True, vmem_limit_bytes=60 * 2**20
        ),
    )(requests, request_adapter[None], adapter_position[None], output_weight, down, up)


def shards(
    requests, output_weight, adapter_down_bank, adapter_up_bank, request_adapter, adapter_position
):
    arguments = (
        requests, output_weight, adapter_down_bank, adapter_up_bank, request_adapter, adapter_position
    )
    rows, width = requests.shape
    owners, pieces = lax.axis_size("owner"), lax.axis_size("tensor")
    bank, rank = adapter_down_bank.shape[0], adapter_down_bank.shape[2]
    cap = max(2, (2 * rows + owners - 1) // owners)
    fits = (
        owners == pieces
        and output_weight.shape[1] % 1024 == 0
        and 2 * rank == LANES
        and bank * rank % LANES == 0
        and rows % 16 == 0
        and cap % 8 == 0
        and cap <= LANES
        and owners * max(bank, cap) <= 256
        and adapter_position.shape[0] <= owners * bank
    )
    return fused(*arguments) if fits else general(*arguments)


def solution(mesh):
    placed = (
        P(("groups", "owner"), "tensor"),
        P("tensor", "owner"),
        P(("groups", "owner"), "tensor", None),
        P(("groups", "owner"), None, "tensor"),
        P(("groups", "owner")),
        P("groups"),
    )
    return jax.shard_map(
        shards,
        mesh=mesh,
        in_specs=placed,
        out_specs=P(("groups", "owner"), "tensor"),
        check_vma=False,
    )
```
